32 devices in a mesh: space: 8 (over z, x), rep: 4 (over y, core).
Axes of the slice: x: 2, y: 2, z: 4, core: 2. Of those that a mesh axis runs over, the one named last changes fastest.
Arguments:
- atom_features: float32 [32768, 64], P('space'), may hold values from -6 to 6
- bond_features: bfloat16 [32768, 1024], P(('space', 'rep')), may hold values from -6 to 6
- offsets: int32 [32768, 16], P(('space', 'rep')), may hold values from -2048 to 2048, as said below
- counts: int32 [32768], P(('space', 'rep')), may hold values from 8 to 16
- cosines: float32 [32768, 256], P(('space', 'rep')), may hold values from -1 to 1
- weight_core: bfloat16 [2, 192, 192], replicated, may hold values from -0.4375 to 0.4375
- weight_atom: bfloat16 [2, 64, 64], replicated, may hold values from -0.75 to 0.75
- weight_pair: bfloat16 [2, 64, 128], replicated, may hold values from -0.75 to 0.75
- weight_cosine: float32 [2, 64], replicated, may hold values from -6 to 6
- weight_bond: bfloat16 [2, 64, 64], replicated, may hold values from -0.75 to 0.75
- weight_energy: float32 [64], replicated, may hold values from -0.75 to 0.75
Outputs:
- atoms_out: float32 [32768, 64], P(('space', 'rep'))
- bonds_out: bfloat16 [32768, 1024], P(('space', 'rep'))
- energy: float32 [], replicated
The draws below stay inside these ranges and needn't reach their ends.
Inputs may be any that keep to these rules, and one draw needn't show every extreme that they name: `offsets`: never zero; |offset| is at most 2048.
All inputs are finite; a program needn't handle non-finite values.
Results may differ from the reference program's by a relative error of at most 0.0045.
Values may be sent and summed in bfloat16 or wider, within the bound.
No kernel may reach another device: no remote copies, remote signals or barrier semaphores. Data moves between devices by JAX's collectives and lax.ppermute only.
A program may use at most 64 MiB of HBM per device.

```python
import math
import jax
import jax.numpy as jnp
from jax import lax

C = 64
SLOT = 16
LAYERS = 2
HALO = 2048
ATOMS = 32768


def draw_offsets(key, part):
    first, second = jax.random.split(jax.random.fold_in(key, 7))
    magnitude = jax.random.randint(first, (ATOMS, SLOT), 1, HALO + 1, dtype=jnp.int32)
    signs = jax.random.randint(second, (ATOMS, SLOT), 0, 2, dtype=jnp.int32) * 2 - 1
    return (magnitude * signs).astype(jnp.int32)


def touch_ends(result, own_key, least, largest):
    longest = result.shape.index(max(result.shape))
    spots = []
    for shift in (0, 1):
        where = [jax.random.randint(jax.random.fold_in(own_key, axis), (), 0, length) for axis, length in enumerate(result.shape)]
        where[longest] = (where[longest] + shift) % result.shape[longest]
        spots.append(tuple(where))
    return result.at[spots[0]].set(least).at[spots[1]].set(largest)


def shard_levels(rng, dims, shards, smallest, largest):
    def one(axis_at, parts):
        steps = jax.random.uniform(jax.random.fold_in(jax.random.fold_in(rng, 6), axis_at), (parts,), jnp.float32, smallest / len(shards), largest / len(shards))
        return jnp.repeat(jnp.exp(steps), dims[axis_at] // parts).reshape((-1,) + (1,) * (len(dims) - axis_at - 1))

    loudness = one(*shards[0])
    for cut in shards[1:]:
        loudness = loudness * one(*cut)
    return loudness


def noise(own_key, shape, deviation, bound, shards=(), held_as=jnp.bfloat16):
    gain = shard_levels(own_key, shape, shards, -0.22, 0.18) if shards else 1.0
    entries = jax.random.normal(own_key, shape, jnp.float32) * deviation * gain
    return jnp.minimum(jnp.maximum(entries, -bound), bound).astype(held_as)


def setup_inputs(seed: int = 0) -> dict:
    key_of = jax.random.split(jax.random.key(seed), 12)
    return {
        "atom_features": noise(key_of[0], (ATOMS, C), 1.0, 6.0, ((0, 8),), jnp.float32),
        "bond_features": noise(key_of[1], (ATOMS, SLOT * C), 1.0, 6.0, ((0, 32),)),
        "offsets": draw_offsets(jax.random.fold_in(key_of[11], 71), 0),
        "counts": touch_ends(jax.random.randint(key_of[3], (ATOMS,), 8, 17), jax.random.fold_in(key_of[3], 1), 8, 16).astype(jnp.int32),
        "cosines": jnp.clip(jax.random.uniform(key_of[4], (ATOMS, SLOT * SLOT), jnp.float32, -1.0, 1.0) * shard_levels(key_of[4], (ATOMS, SLOT * SLOT), ((0, 32),), -0.4, 0.0), -1.0, 1.0),
        "weight_core": noise(key_of[5], (LAYERS, 3 * C, 3 * C), (3 * C) ** -0.5, 0.4375),
        "weight_atom": noise(key_of[6], (LAYERS, C, C), C ** -0.5, 0.75),
        "weight_pair": noise(key_of[7], (LAYERS, C, 2 * C), C ** -0.5, 0.75),
        "weight_cosine": noise(key_of[8], (LAYERS, C), 1.0, 6.0, (), jnp.float32),
        "weight_bond": noise(key_of[9], (LAYERS, C, C), C ** -0.5, 0.75),
        "weight_energy": noise(key_of[10], (C,), C ** -0.5, 0.75, (), jnp.float32),
    }


def interact(h_rows, neighbours, e_rows, cnt_rows, cos_rows, weight_core, weight_atom, weight_pair, weight_cosine, weight_bond):
    row_count = h_rows.shape[0]
    channels = h_rows.shape[1]
    slot_count = e_rows.shape[1] // channels
    bond_rows = e_rows.reshape(row_count, slot_count, channels)
    centre = jnp.broadcast_to(h_rows.astype(jnp.bfloat16)[:, None, :], (row_count, slot_count, channels))
    joined = jnp.concatenate([centre, neighbours, bond_rows], axis=2).reshape(row_count * slot_count, 3 * channels)
    mixed_all = jnp.dot(joined, weight_core, preferred_element_type=jnp.float32).reshape(row_count, slot_count, 3 * channels)
    live_mask = (jnp.arange(slot_count, dtype=jnp.int32)[None, :] < cnt_rows[:, None]).astype(jnp.float32)
    inverse_count = 1.0 / cnt_rows.astype(jnp.float32)
    message = jax.nn.sigmoid(mixed_all[..., :channels]) * jax.nn.silu(mixed_all[..., channels:2 * channels]) * live_mask[..., None]
    summed = (lax.optimization_barrier(jnp.sum(message, axis=1)) * inverse_count[:, None]).astype(jnp.bfloat16)
    atom_next = h_rows + jnp.dot(summed, weight_atom, preferred_element_type=jnp.float32)
    paired = jnp.dot(bond_rows.reshape(row_count * slot_count, channels), weight_pair, preferred_element_type=jnp.float32).reshape(row_count, slot_count, 2 * channels)
    cosine_tile = cos_rows.reshape(row_count, slot_count, slot_count)
    angle_input = paired[:, :, None, :channels] + paired[:, None, :, channels:] + cosine_tile[..., None] * weight_cosine
    pair_mask = live_mask[:, :, None] * live_mask[:, None, :] * (1.0 - jnp.eye(slot_count, dtype=jnp.float32))
    angular = (lax.optimization_barrier(jnp.sum(jax.nn.silu(angle_input) * pair_mask[..., None], axis=2)) * inverse_count[:, None, None]).astype(jnp.bfloat16)
    update = jnp.dot(angular.reshape(row_count * slot_count, channels), weight_bond, preferred_element_type=jnp.float32).reshape(row_count, slot_count, channels)
    update = update * jax.nn.sigmoid(mixed_all[..., 2 * channels:]) * live_mask[..., None]
    bond_next = (bond_rows.astype(jnp.float32) + update).astype(jnp.bfloat16).reshape(row_count, slot_count * channels)
    return (atom_next, bond_next)

def reference(atom_features, bond_features, offsets, counts, cosines, weight_core, weight_atom, weight_pair, weight_cosine, weight_bond, weight_energy):
    total = atom_features.shape[0]
    block_rows = math.gcd(total, 1024)
    number = total // block_rows
    state = atom_features
    bonds_now = bond_features
    starts = jnp.arange(number, dtype=jnp.int32) * block_rows
    for layer_index in range(LAYERS):
        atom_table = state.astype(jnp.bfloat16)

        def block_step(items):
            block_start, h_rows, e_rows, off_rows, cnt_rows, cos_rows = items
            positions = block_start + jnp.arange(block_rows, dtype=jnp.int32)
            neighbour_ids = ((positions[:, None] + off_rows) % total).astype(jnp.int32)
            neighbours = jnp.take(atom_table, neighbour_ids, axis=0)
            return interact(h_rows, neighbours, e_rows, cnt_rows, cos_rows, weight_core[layer_index], weight_atom[layer_index], weight_pair[layer_index], weight_cosine[layer_index], weight_bond[layer_index])
        atom_next, bond_next = lax.map(block_step, (starts, state.reshape(number, block_rows, -1), bonds_now.reshape(number, block_rows, -1), offsets.reshape(number, block_rows, -1), counts.reshape(number, block_rows), cosines.reshape(number, block_rows, -1)))
        state = atom_next.reshape(total, -1)
        bonds_now = bond_next.reshape(total, -1)
    energy = jnp.sum(state * weight_energy) / math.sqrt(total)
    return (state, bonds_now, energy)
```

```python
import functools
import math

import jax
import jax.numpy as jnp
from jax import lax
from jax.experimental import pallas as pl
from jax.experimental.pallas import tpu as pltpu
from jax.sharding import PartitionSpec as P

LAYERS = 2
LANES = 256
DEAD = -1e30
VMEM = pl.BlockSpec(memory_space=pltpu.VMEM)


def tree_push(stack, term):
    level = 0
    while stack and stack[-1][0] == level:
        term = term + stack.pop()[1]
        level += 1
    stack.append((level, term))


def tree_total(stack):
    total = stack.pop()[1]
    while stack:
        total = total + stack.pop()[1]
    return total


def layer_kernel(
    first,
    last,
    slots,
    channels,
    pieces,
    *refs,
):
    piece_refs = refs[:pieces]
    (state_ref, bond_ref, off_ref, cnt_ref, cos_ref, core_ref, atom_ref, pair_ref, wcos_ref, wbond_ref) = refs[
        pieces : pieces + 10
    ]
    rest = refs[pieces + 10 :]
    if last:
        energy_ref, atoms_out, bonds_out, energy_out = rest[:4]
        rest = rest[4:]
    else:
        atoms_out, table_out, bonds_out, cos_out = rest[:4]
        rest = rest[4:]
    tab, core_t, pair_t, atom_t, bond_t, wc, p_s, q_s, n_s, msg_s, new_s, cos_s, bond_s = rest
    blocks = off_ref.shape[0]
    per_piece = blocks
    reach = tab.shape[0] - blocks + 1
    bf = jnp.bfloat16
    f32 = jnp.float32
    for index in range(pieces):
        tab[index * per_piece : (index + 1) * per_piece] = piece_refs[index][...]
    core_t[...] = (core_ref[...].astype(f32).T * 0.5).astype(bf)
    pair_t[...] = (pair_ref[...].astype(f32).T * 0.5).astype(bf)
    atom_t[...] = atom_ref[...].astype(f32).T.astype(bf)
    bond_t[...] = (wbond_ref[...].astype(f32).T * 0.5).astype(bf)
    wc[...] = jnp.broadcast_to((wcos_ref[...] * 0.5).T, wc.shape).astype(bf)
    columns = lax.broadcasted_iota(jnp.int32, (LANES, LANES), 0)
    lane = lax.broadcasted_iota(jnp.int32, (1, LANES), 1)
    centre = pieces // 2 * per_piece

    def block(b, carry):
        rows = pl.ds(pl.multiple_of(b * LANES, LANES), LANES)
        count = cnt_ref[b]
        own = tab[centre + b]

        if first:
            cos_s[...] = cos_ref[rows, :].T
            cos_out[b] = cos_s[...].astype(cos_out.dtype)
            for pair in range(slots // 2):
                both = bond_ref[rows, pair * 2 * channels : (pair + 1) * 2 * channels].astype(f32).T.astype(bf)
                bond_s[2 * pair] = both[:channels]
                bond_s[2 * pair + 1] = both[channels:]
        else:
            cos_s[...] = cos_ref[b]

        def bond_at(k):
            return bond_s[k] if first else bond_ref[b, k]

        def project(k, carry):
            both = jnp.dot(pair_t[...], bond_at(k), preferred_element_type=f32)
            p_s[k] = both[:channels].astype(bf)
            q_s[k] = jnp.where(k < count, both[channels:], DEAD).astype(bf)
            return carry

        lax.fori_loop(0, slots, project, 0, unroll=4)

        def gather(k):
            index = off_ref[b, pl.ds(k, 1), :] + (lane + (reach - 1) // 2 * LANES)
            low = index % LANES
            high = index // LANES
            chosen = jnp.where(columns == low, 1.0, 0.0).astype(bf)
            lhs = tab[pl.ds(b, reach)].reshape(reach * channels, LANES)
            picked = jnp.dot(lhs, chosen, preferred_element_type=f32)
            result = picked[:channels]
            for h in range(1, reach):
                result = jnp.where(high == h, picked[h * channels : (h + 1) * channels], result)
            return result.astype(bf)

        n_s[0] = gather(0)
        msg_s[...] = jnp.zeros_like(msg_s)

        def slot(j, carry):
            live = jnp.where(j < count, 1.0, 0.0)
            here = bond_at(j)
            joined = jnp.concatenate([own, n_s[j % 2], here], axis=0)
            mixed = jnp.dot(core_t[...], joined, preferred_element_type=f32)
            n_s[(j + 1) % 2] = gather(jnp.minimum(j + 1, slots - 1))
            gates = jnp.tanh(mixed)
            cores = mixed[channels : 2 * channels]
            msg_s[...] += (1.0 + gates[:channels]) * (cores + cores * gates[channels : 2 * channels]) * live
            p = p_s[j]
            stack = []
            for m in range(1, slots):
                k = (j + m) % slots
                cosine = jnp.broadcast_to(cos_s[pl.ds(j * slots + k, 1), :], (8, LANES)).astype(bf)
                cosine = jnp.concatenate([cosine] * (channels // 8), axis=0)
                y = p + (q_s[k] + cosine * wc[...])
                tree_push(stack, y + y * jnp.tanh(y))
            angular = (tree_total(stack).astype(f32) * (1.0 / count.astype(f32))).astype(bf)
            update = jnp.dot(bond_t[...], angular, preferred_element_type=f32)
            update = update * (1.0 + gates[2 * channels :]) * live
            fresh = (here.astype(f32) + update).astype(bf)
            if last:
                new_s[j] = fresh
            else:
                bonds_out[b, j] = fresh
            return carry

        lax.fori_loop(0, slots, slot, 0)
        summed = (msg_s[...] * (0.5 / count.astype(f32))).astype(bf)
        state = (state_ref[b]) + jnp.dot(atom_t[...], summed, preferred_element_type=f32)
        if last:
            atoms_out[rows, :] = state.T
            energy_out[b] = jnp.sum(state * energy_ref[...].T, axis=0, keepdims=True)
            for pair in range(slots // 2):
                both = jnp.concatenate([new_s[2 * pair], new_s[2 * pair + 1]], axis=0)
                bonds_out[rows, pair * 2 * channels : (pair + 1) * 2 * channels] = both.astype(f32).T.astype(bf)
        else:
            atoms_out[b] = state
            table_out[b] = state.astype(bf)
        return carry

    lax.fori_loop(0, blocks, block, 0)


def run_layer(first, last, tables, state, bonds, offs, counts, cosines, weights, energy):
    blocks, slots = offs.shape[:2]
    channels = state.shape[1]
    quarter = blocks * LANES
    bf = jnp.bfloat16
    f32 = jnp.float32
    sds = jax.ShapeDtypeStruct
    if last:
        outs = [
            sds((quarter, channels), f32),
            sds((quarter, slots * channels), bf),
            sds((blocks, 1, LANES), f32),
        ]
    else:
        outs = [
            sds((blocks, channels, LANES), f32),
            sds((blocks, channels, LANES), bf),
            sds((blocks, slots, channels, LANES), bf),
            sds((blocks, slots * slots, LANES), f32),
        ]
    operands = [*tables, state, bonds, offs, counts, cosines, *weights]
    if last:
        operands.append(energy)
    return pl.pallas_call(
        functools.partial(layer_kernel, first, last, slots, channels, len(tables)),
        out_shape=outs,
        in_specs=[VMEM] * len(operands),
        out_specs=[VMEM] * len(outs),
        scratch_shapes=[
            pltpu.VMEM((blocks * len(tables), channels, LANES), bf),
            pltpu.VMEM((3 * channels, 3 * channels), bf),
            pltpu.VMEM((2 * channels, channels), bf),
            pltpu.VMEM((channels, channels), bf),
            pltpu.VMEM((channels, channels), bf),
            pltpu.VMEM((channels, LANES), bf),
            pltpu.VMEM((slots, channels, LANES), bf),
            pltpu.VMEM((slots, channels, LANES), bf),
            pltpu.VMEM((2, channels, LANES), bf),
            pltpu.VMEM((channels, LANES), f32),
            pltpu.VMEM((slots, channels, LANES), bf),
            pltpu.VMEM((slots * slots, LANES), f32),
            pltpu.VMEM((slots, channels, LANES), bf),
        ],
        compiler_params=pltpu.CompilerParams(vmem_limit_bytes=56 * 2**20),
    )(*operands)


def passed_along(value, axis, steps):
    count = lax.axis_size(axis)
    return lax.ppermute(value, axis, [(source, (source + steps) % count) for source in range(count)])


def around(table):
    return [table if steps == 0 else passed_along(table, ("space", "rep"), steps) for steps in (2, 1, 0, -1, -2)]


def per_device(
    atom_features,
    bond_features,
    offsets,
    counts,
    cosines,
    weight_core,
    weight_atom,
    weight_pair,
    weight_cosine,
    weight_bond,
    weight_energy,
):
    quarter, slots = offsets.shape
    domain, channels = atom_features.shape
    blocks = quarter // LANES
    own = lax.dynamic_slice_in_dim(atom_features, lax.axis_index("rep") * quarter, quarter, 0)
    state = own.reshape(blocks, LANES, channels).transpose(0, 2, 1)
    table = state.astype(jnp.bfloat16)
    offs = offsets.reshape(blocks, LANES, slots).transpose(0, 2, 1)
    cnts = counts.reshape(blocks, 1, LANES)
    bonds = bond_features
    energy = None
    for layer in range(LAYERS):
        weights = (
            weight_core[layer],
            weight_atom[layer],
            weight_pair[layer],
            weight_cosine[layer : layer + 1],
            weight_bond[layer],
        )
        last = layer == LAYERS - 1
        outs = run_layer(
            layer == 0, last, around(table), state, bonds, offs, cnts, cosines, weights, weight_energy[None, :]
        )
        if last:
            state, bonds, energy = outs
        else:
            state, table, bonds, cosines = outs
    total = lax.psum(jnp.sum(energy), ("space", "rep"))
    return (state, bonds, total / math.sqrt(lax.axis_size("space") * domain))


def solution(mesh):
    return jax.shard_map(
        per_device,
        mesh=mesh,
        in_specs=(
            P("space", None),
            P(("space", "rep"), None),
            P(("space", "rep"), None),
            P(("space", "rep")),
            P(("space", "rep"), None),
            P(),
            P(),
            P(),
            P(),
            P(),
            P(),
        ),
        out_specs=(P(("space", "rep"), None), P(("space", "rep"), None), P()),
        check_vma=False,
    )
```

```python
import functools
import math

import jax
import jax.numpy as jnp
from jax import lax
from jax.experimental import pallas as pl
from jax.experimental.pallas import tpu as pltpu
from jax.sharding import PartitionSpec as P

LAYERS = 2
LANES = 256
DEAD = -1e30
BATCH = 4
BF = jnp.bfloat16
F32 = jnp.float32
AXES = ("space", "rep")
PARAMS = pltpu.CompilerParams(vmem_limit_bytes=56 * 2**20, dimension_semantics=("arbitrary",))


def tree_push(stack, term):
    level = 0
    while stack and stack[-1][0] == level:
        term = term + stack.pop()[1]
        level += 1
    stack.append((level, term))


def tree_total(stack):
    total = stack.pop()[1]
    while stack:
        total = total + stack.pop()[1]
    return total


def gather_kernel(layer, first, last, slots, channels, quarter, *refs):
    refs = list(refs)
    b = pl.program_id(0)
    per = quarter // LANES
    rim = 2 * per
    reach = 2 * rim + 1
    if first:
        domain_ref, far_ref = refs[:2]
        refs = refs[2:]
    else:
        piece_refs = refs[:5]
        state_ref = refs[5]
        refs = refs[6:]
    bond_ref, off_ref, cnt_ref, core_ref, atom_ref = refs[:5]
    refs = refs[5:]
    if last:
        energy_w_ref = refs.pop(0)
    state_out, gate_out = refs[:2]
    refs = refs[2:]
    if not last:
        table_out = refs.pop(0)
    if first:
        bonds_out = refs.pop(0)
    if last:
        energy_out = refs.pop(0)
    tab, core_t, atom_t, n_s, msg_s = refs

    @pl.when(b == 0)
    def _():
        core_t[...] = (core_ref[layer].astype(F32).T * 0.5).astype(BF)
        atom_t[...] = atom_ref[layer].astype(F32).T.astype(BF)
        if first:
            inner = domain_ref.shape[1] // LANES
            for i in range(inner):
                tab[rim + i] = domain_ref[:, i * LANES : (i + 1) * LANES].astype(BF)
            for i in range(rim):
                part = far_ref[:, i * LANES : (i + 1) * LANES]
                tab[i] = part
                tab[rim + inner + i] = part
        else:
            for piece, ref in enumerate(piece_refs):
                for i in range(per):
                    tab[piece * per + i] = ref[:, i * LANES : (i + 1) * LANES]
        if last:
            energy_out[...] = jnp.zeros_like(energy_out)

    if first:
        base = lax.axis_index("rep") * per + b
        state = domain_ref[:, pl.ds(pl.multiple_of(base * LANES, LANES), LANES)]
        for pair in range(slots // 2):
            both = bond_ref[:, pair * 2 * channels : (pair + 1) * 2 * channels].astype(F32).T.astype(BF)
            bonds_out[2 * pair] = both[:channels]
            bonds_out[2 * pair + 1] = both[channels:]
        bonds = bonds_out
    else:
        base = b
        state = state_ref[...]
        bonds = bond_ref

    own = tab[base + rim]
    count = cnt_ref[...]
    columns = lax.broadcasted_iota(jnp.int32, (LANES, LANES), 0)
    lane = lax.broadcasted_iota(jnp.int32, (1, LANES), 1) + rim * LANES

    def gather(group):
        for u in range(BATCH):
            index = off_ref[pl.ds(group * BATCH + u, 1), :] + lane
            low = index % LANES
            high = index // LANES
            chosen = jnp.where(columns == low, 1.0, 0.0).astype(BF)
            lhs = tab[pl.ds(base, reach)].reshape(reach * channels, LANES)
            picked = jnp.dot(lhs, chosen, preferred_element_type=F32)
            result = picked[:channels]
            for h in range(1, reach):
                result = jnp.where(high == h, picked[h * channels : (h + 1) * channels], result)
            n_s[group * BATCH + u] = result.astype(BF)

    def gates(group):
        total = msg_s[...] if group else None
        for u in range(BATCH):
            j = group * BATCH + u
            live = jnp.where(j < count, 1.0, 0.0)
            joined = jnp.concatenate([own, n_s[j], bonds[j]], axis=0)
            mixed = jnp.dot(core_t[...], joined, preferred_element_type=F32)
            gate = jnp.tanh(mixed)
            cores = mixed[channels : 2 * channels]
            message = (1.0 + gate[:channels]) * (cores + cores * gate[channels : 2 * channels]) * live
            total = message if total is None else total + message
            gate_out[j] = ((1.0 + gate[2 * channels :]) * live).astype(BF)
        msg_s[...] = total

    groups = slots // BATCH
    gather(0)
    for group in range(1, groups):
        gather(group)
        gates(group - 1)
    gates(groups - 1)
    summed = (msg_s[...] * (0.5 / count.astype(F32))).astype(BF)
    state = state + jnp.dot(atom_t[...], summed, preferred_element_type=F32)
    state_out[...] = state
    if not last:
        table_out[...] = state.astype(BF)
    if last:
        energy_out[...] += jnp.sum(state * energy_w_ref[...].T, axis=0, keepdims=True)


def whole(array):
    return pl.BlockSpec(array.shape, lambda b: (0,) * len(array.shape))


def run_gather(layer, tables, state, bonds, offs, counts, weights, energy):
    first, last = layer == 0, layer == LAYERS - 1
    slots, quarter = offs.shape
    channels = weights[1].shape[1]
    per = quarter // LANES
    column = pl.BlockSpec((channels, LANES), lambda b: (0, b))
    slab = pl.BlockSpec((None, slots, channels, LANES), lambda b: (b, 0, 0, 0))
    sds = jax.ShapeDtypeStruct
    operands = list(tables)
    specs = [whole(x) for x in tables]
    if not first:
        operands.append(state)
        specs.append(column)
    operands += [bonds, offs, counts, *weights]
    specs += [
        pl.BlockSpec((LANES, slots * channels), lambda b: (b, 0)) if first else slab,
        pl.BlockSpec((slots, LANES), lambda b: (0, b)),
        pl.BlockSpec((1, LANES), lambda b: (0, b)),
        *[whole(x) for x in weights],
    ]
    outs = [sds((channels, quarter), F32), sds((per, slots, channels, LANES), BF)]
    out_specs = [column, slab]
    if last:
        operands.append(energy)
        specs.append(whole(energy))
    if not last:
        outs.append(sds((channels, quarter), BF))
        out_specs.append(column)
    if first:
        outs.append(sds((per, slots, channels, LANES), BF))
        out_specs.append(slab)
    if last:
        outs.append(sds((1, LANES), F32))
        out_specs.append(pl.BlockSpec((1, LANES), lambda b: (0, 0)))
    rows = (tables[0].shape[1] // LANES + 4 * per) if first else 5 * per
    return pl.pallas_call(
        functools.partial(gather_kernel, layer, first, last, slots, channels, quarter),
        grid=(per,),
        out_shape=outs,
        in_specs=specs,
        out_specs=out_specs,
        scratch_shapes=[
            pltpu.VMEM((rows, channels, LANES), BF),
            pltpu.VMEM((3 * channels, 3 * channels), BF),
            pltpu.VMEM((channels, channels), BF),
            pltpu.VMEM((slots, channels, LANES), BF),
            pltpu.VMEM((channels, LANES), F32),
        ],
        compiler_params=PARAMS,
        cost_estimate=pl.CostEstimate(flops=10 * 2**30, bytes_accessed=2**23, transcendentals=2**22),
    )(*operands)


def angle_kernel(layer, first, last, slots, channels, *refs):
    refs = list(refs)
    bond_ref, gate_ref, cnt_ref, cos_ref, pair_ref, wcos_ref, wbond_ref = refs[:7]
    refs = refs[7:]
    if last:
        refs.pop(0)
    bonds_out = refs.pop(0)
    if first:
        cos_out = refs.pop(0)
    pair_t, bond_t, wc, p_s, q_s, a_s, new_s = refs

    @pl.when(pl.program_id(0) == 0)
    def _():
        pair_t[...] = (pair_ref[layer].astype(F32).T * 0.5).astype(BF)
        bond_t[...] = (wbond_ref[layer].astype(F32).T * 0.5).astype(BF)
        wc[...] = jnp.broadcast_to((wcos_ref[layer : layer + 1] * 0.5).T, wc.shape).astype(BF)

    count = cnt_ref[...]
    inverse = 1.0 / count.astype(F32)
    if first:
        cos_out[...] = cos_ref[...].T
        cosines = cos_out
    else:
        cosines = cos_ref

    for k in range(slots):
        both = jnp.dot(pair_t[...], bond_ref[k], preferred_element_type=F32)
        p_s[k] = both[:channels].astype(BF)
        q_s[k] = jnp.where(k < count, both[channels:], DEAD).astype(BF)

    fresh = new_s if last else bonds_out

    def update(j):
        change = jnp.dot(bond_t[...], a_s[j], preferred_element_type=F32)
        fresh[j] = (bond_ref[j].astype(F32) + change * gate_ref[j].astype(F32)).astype(BF)

    def slot(j, carry):
        p = p_s[j]
        stack = []
        for m in range(1, slots):
            k = (j + m) % slots
            cosine = jnp.broadcast_to(cosines[pl.ds(j * slots + k, 1), :], (8, LANES)).astype(BF)
            cosine = jnp.concatenate([cosine] * (channels // 8), axis=0)
            y = p + (q_s[k] + cosine * wc[...])
            tree_push(stack, y + y * jnp.tanh(y))
        a_s[j] = (tree_total(stack).astype(F32) * inverse).astype(BF)
        return carry

    lax.fori_loop(0, slots, slot, 0)
    for j in range(slots):
        update(j)
    if last:
        for pair in range(slots // 2):
            both = jnp.concatenate([new_s[2 * pair], new_s[2 * pair + 1]], axis=0)
            bonds_out[:, pair * 2 * channels : (pair + 1) * 2 * channels] = both.astype(F32).T.astype(BF)


def run_angle(layer, part, buffer, bonds, gates, counts, cosines, weights):
    first, last = layer == 0, layer == LAYERS - 1
    per, slots, channels = bonds.shape[:3]
    at = (lambda b: b) if part is None else (lambda b: b + part)
    steps = per if part is None else 1
    slab = pl.BlockSpec((None, slots, channels, LANES), lambda b: (at(b), 0, 0, 0))
    tile = pl.BlockSpec((None, slots * slots, LANES), lambda b: (at(b), 0, 0))
    sds = jax.ShapeDtypeStruct
    operands = [bonds, gates, counts, cosines, *weights]
    specs = [
        slab,
        slab,
        pl.BlockSpec((1, LANES), lambda b: (0, at(b))),
        pl.BlockSpec((LANES, slots * slots), lambda b: (at(b), 0)) if first else tile,
        *[whole(x) for x in weights],
    ]
    aliases = {}
    if last:
        outs = [sds((per * LANES, slots * channels), BF)]
        out_specs = [pl.BlockSpec((LANES, slots * channels), lambda b: (at(b), 0))]
        if buffer is None:
            buffer = jnp.zeros((8, 128), F32)
        else:
            aliases = {len(operands): 0}
        operands.append(buffer)
        specs.append(pl.BlockSpec(memory_space=pl.ANY))
    else:
        outs = [sds((per, slots, channels, LANES), BF), sds((per, slots * slots, LANES), F32)]
        out_specs = [slab, tile]
    return pl.pallas_call(
        functools.partial(angle_kernel, layer, first, last, slots, channels),
        grid=(steps,),
        out_shape=outs,
        in_specs=specs,
        out_specs=out_specs,
        input_output_aliases=aliases,
        scratch_shapes=[
            pltpu.VMEM((2 * channels, channels), BF),
            pltpu.VMEM((channels, channels), BF),
            pltpu.VMEM((channels, LANES), BF),
            pltpu.VMEM((slots, channels, LANES), BF),
            pltpu.VMEM((slots, channels, LANES), BF),
            pltpu.VMEM((slots, channels, LANES), BF),
            pltpu.VMEM((slots, channels, LANES), BF),
        ],
        compiler_params=PARAMS,
        cost_estimate=pl.CostEstimate(flops=2**30 * steps, bytes_accessed=2**21 * steps, transcendentals=2**22 * steps),
    )(*operands)


def passed_along(value, steps):
    count = lax.axis_size(AXES)
    return lax.ppermute(value, AXES, [(source, (source + steps) % count) for source in range(count)])


def far_side(domain, quarter):
    rim = 2 * quarter
    rep = lax.axis_size("rep")
    total = lax.axis_size(AXES)
    payload = jnp.where(lax.axis_index("rep") < 2, domain[:, :rim], domain[:, -rim:]).astype(BF)
    pairs = []
    for start in range(0, total, rep):
        for d in range(2):
            pairs.append(((start + d - 2) % total, start + d))
            pairs.append(((start + rep + d) % total, start + rep - 2 + d))
    return lax.ppermute(payload, AXES, pairs)


def sum_stages():
    rep, space = lax.axis_size("rep"), lax.axis_size("space")

    def over_rep(value):
        moved = [
            lax.ppermute(value, "rep", [(i, (i + s) % rep) for i in range(rep)]) for s in range(1, rep)
        ]
        return sum(moved, value)

    def over_space(step):
        return lambda value: value + lax.ppermute(value, "space", [(i, i ^ step) for i in range(space)])

    return [over_rep] + [over_space(1 << s) for s in range(space.bit_length() - 1)]


def per_device(
    atom_features,
    bond_features,
    offsets,
    counts,
    cosines,
    weight_core,
    weight_atom,
    weight_pair,
    weight_cosine,
    weight_bond,
    weight_energy,
):
    quarter = offsets.shape[0]
    per = quarter // LANES
    domain = atom_features.T
    offs = offsets.T
    cnts = counts[None, :]
    into_atoms = (weight_core, weight_atom)
    into_bonds = (weight_pair, weight_cosine, weight_bond)
    far = far_side(domain, quarter)
    state, gates, table, bonds = run_gather(
        0, [domain, far], None, bond_features, offs, cnts, into_atoms, None
    )
    pieces = [table if s == 0 else passed_along(table, s) for s in (2, 1, 0, -1, -2)]
    bonds, tiles = run_angle(0, None, None, bonds, gates, cnts, cosines, into_bonds)
    state, gates, energy = run_gather(1, pieces, state, bonds, offs, cnts, into_atoms, weight_energy[None, :])
    stages = sum_stages()
    out = None
    for part in range(per):
        if stages:
            energy = stages.pop(0)(energy)
        (out,) = run_angle(1, part, out, bonds, gates, cnts, tiles, into_bonds)
    for stage in stages:
        energy = stage(energy)
    scale = math.sqrt(lax.axis_size("space") * domain.shape[1])
    return (state.T, out, jnp.sum(energy) / scale)


def solution(mesh):
    return jax.shard_map(
        per_device,
        mesh=mesh,
        in_specs=(
            P("space", None),
            P(("space", "rep"), None),
            P(("space", "rep"), None),
            P(("space", "rep")),
            P(("space", "rep"), None),
            P(),
            P(),
            P(),
            P(),
            P(),
            P(),
        ),
        out_specs=(P(("space", "rep"), None), P(("space", "rep"), None), P()),
        check_vma=False,
    )
```

```python
import functools
import math

import jax
import jax.numpy as jnp
from jax import lax
from jax.experimental import pallas as pl
from jax.experimental.pallas import tpu as pltpu
from jax.sharding import PartitionSpec as P

LAYERS = 2
LANES = 256
DEAD = -1e30
BATCH = 4
BF = jnp.bfloat16
F32 = jnp.float32
AXES = ("space", "rep")
PARAMS = pltpu.CompilerParams(vmem_limit_bytes=24 * 2**20)
VMEM = pl.BlockSpec(memory_space=pltpu.VMEM)
ANY = pl.BlockSpec(memory_space=pl.ANY)


def tree_push(stack, term):
    level = 0
    while stack and stack[-1][0] == level:
        term = term + stack.pop()[1]
        level += 1
    stack.append((level, term))


def tree_total(stack):
    total = stack.pop()[1]
    while stack:
        total = total + stack.pop()[1]
    return total


def bond_update(weight, angular, bond, gate):
    change = jnp.dot(weight, angular, preferred_element_type=F32)
    return (bond.astype(F32) + change * gate).astype(BF)


def block_lanes(b):
    return pl.ds(pl.multiple_of(b * LANES, LANES), LANES)


def gather_kernel(layer, first, last, slots, channels, quarter, *refs):
    refs = list(refs)
    per = quarter // LANES
    rim = 2 * per
    reach = 2 * rim + 1
    if first:
        state_ref, far_ref = refs[:2]
        refs = refs[2:]
    else:
        piece_refs = refs[:5]
        state_ref = refs[5]
        refs = refs[6:]
    bond_ref, off_ref, cnt_ref, core_ref, atom_ref = refs[:5]
    refs = refs[5:]
    if last:
        energy_w_ref = refs.pop(0)
        refs.pop(0)
    else:
        angular_ref, wbond_ref = refs[:2]
        refs = refs[2:]
    state_out = refs.pop(0)
    if last:
        gate_out, energy_out = refs[:2]
        energy_out[...] = jnp.zeros_like(energy_out)
        energy_w = energy_w_ref[...].T
    else:
        table_out, bonds_out = refs[:2]
    refs = refs[2:]
    tab, core_t, atom_t, bond_t, n_s, msg_s = refs
    core_t[...] = (core_ref[layer].astype(F32).T * 0.5).astype(BF)
    atom_t[...] = atom_ref[layer].astype(F32).T.astype(BF)
    if not last:
        bond_t[...] = (wbond_ref[layer].astype(F32).T * 0.5).astype(BF)
    skip = lax.axis_index("rep") * per if first else 0
    if first:
        inner = state_ref.shape[1] // LANES
        for i in range(inner):
            tab[rim + i] = state_ref[:, i * LANES : (i + 1) * LANES].astype(BF)
        for i in range(rim):
            part = far_ref[:, i * LANES : (i + 1) * LANES]
            tab[i] = part
            tab[rim + inner + i] = part
    else:
        for piece, ref in enumerate(piece_refs):
            for i in range(per):
                tab[piece * per + i] = ref[:, i * LANES : (i + 1) * LANES]
    columns = lax.broadcasted_iota(jnp.int32, (LANES, LANES), 0)
    lane = lax.broadcasted_iota(jnp.int32, (1, LANES), 1) + rim * LANES

    def block(b, carry):
        base = skip + b
        here = block_lanes(b)
        own = tab[base + rim]
        count = cnt_ref[:, here]

        def gather(group):
            for j in range(group * BATCH, (group + 1) * BATCH):
                index = off_ref[j : j + 1, here] + lane
                low = index % LANES
                high = index // LANES
                chosen = jnp.where(columns == low, 1.0, 0.0).astype(BF)
                lhs = tab[pl.ds(base, reach)].reshape(reach * channels, LANES)
                picked = jnp.dot(lhs, chosen, preferred_element_type=F32)
                result = picked[:channels]
                for h in range(1, reach):
                    result = jnp.where(high == h, picked[h * channels : (h + 1) * channels], result)
                n_s[j] = result.astype(BF)

        def gates(group):
            total = msg_s[...] if group else None
            for u in range(BATCH):
                j = group * BATCH + u
                live = jnp.where(j < count, 1.0, 0.0)
                bond = bond_ref[b, j]
                joined = jnp.concatenate([own, n_s[j], bond], axis=0)
                mixed = jnp.dot(core_t[...], joined, preferred_element_type=F32)
                gate = jnp.tanh(mixed)
                cores = mixed[channels : 2 * channels]
                message = (1.0 + gate[:channels]) * (cores + cores * gate[channels : 2 * channels]) * live
                total = message if total is None else total + message
                bond_gate = (1.0 + gate[2 * channels :]) * live
                if last:
                    gate_out[b, j] = bond_gate.astype(BF)
                else:
                    bonds_out[b, j] = bond_update(bond_t[...], angular_ref[b, j], bond, bond_gate)
            msg_s[...] = total

        groups = slots // BATCH
        gather(0)
        for group in range(1, groups):
            gather(group)
            gates(group - 1)
        gates(groups - 1)
        summed = (msg_s[...] * (0.5 / count.astype(F32))).astype(BF)
        state = state_ref[:, block_lanes(base) if first else here]
        state = state + jnp.dot(atom_t[...], summed, preferred_element_type=F32)
        state_out[:, here] = state
        if last:
            energy_out[...] += jnp.sum(state * energy_w, axis=0, keepdims=True)
        else:
            table_out[:, here] = state.astype(BF)
        return carry

    lax.fori_loop(0, per, block, 0)


def run_gather(layer, tables, state, bonds, offs, counts, weights, extra):
    first, last = layer == 0, layer == LAYERS - 1
    slots, quarter = offs.shape
    channels = weights[1].shape[1]
    per = quarter // LANES
    sds = jax.ShapeDtypeStruct
    operands = list(tables)
    if not first:
        operands.append(state)
    operands += [bonds, offs, counts, *weights, *extra]
    specs = [VMEM] * len(operands)
    slab = sds((per, slots, channels, LANES), BF)
    if last:
        specs[-1] = ANY
        outs = [sds((channels, quarter), F32), slab, sds((1, LANES), F32)]
    else:
        outs = [sds((channels, quarter), F32), sds((channels, quarter), BF), slab]
    rows = (tables[0].shape[1] // LANES + 4 * per) if first else 5 * per
    return pl.pallas_call(
        functools.partial(gather_kernel, layer, first, last, slots, channels, quarter),
        out_shape=outs,
        in_specs=specs,
        out_specs=[VMEM] * len(outs),
        scratch_shapes=[
            pltpu.VMEM((rows, channels, LANES), BF),
            pltpu.VMEM((3 * channels, 3 * channels), BF),
            pltpu.VMEM((channels, channels), BF),
            pltpu.VMEM((channels, channels), BF),
            pltpu.VMEM((slots, channels, LANES), BF),
            pltpu.VMEM((channels, LANES), F32),
        ],
        compiler_params=PARAMS,
        cost_estimate=pl.CostEstimate(flops=10 * 2**30, bytes_accessed=2**23, transcendentals=2**22),
    )(*operands)


def angle_kernel(layer, first, start, steps, slots, channels, *refs):
    bond_ref, cnt_ref, cos_ref, pair_ref, wcos_ref, angular_out = refs[:6]
    refs = refs[6:]
    if first:
        bonds, cosines, pair_t, wc, p_s, q_s = refs
    else:
        pair_t, wc, p_s, q_s = refs
        bonds, cosines = bond_ref, cos_ref
    pair_t[...] = (pair_ref[layer].astype(F32).T * 0.5).astype(BF)
    wc[...] = jnp.broadcast_to((wcos_ref[layer : layer + 1] * 0.5).T, wc.shape).astype(BF)

    def block(step, carry):
        b = start + step
        count = cnt_ref[:, block_lanes(b)]
        inverse = 1.0 / count.astype(F32)
        if first:
            rows = block_lanes(b)
            cosines[b] = cos_ref[rows, :].T
            for pair in range(slots // 2):
                both = bond_ref[rows, pair * 2 * channels : (pair + 1) * 2 * channels].astype(F32).T.astype(BF)
                bonds[b, 2 * pair] = both[:channels]
                bonds[b, 2 * pair + 1] = both[channels:]

        for k in range(slots):
            both = jnp.dot(pair_t[...], bonds[b, k], preferred_element_type=F32)
            p_s[k] = both[:channels].astype(BF)
            q_s[k] = jnp.where(k < count, both[channels:], DEAD).astype(BF)

        def slot(j, inner):
            p = p_s[j]
            stack = []
            for m in range(1, slots):
                k = (j + m) % slots
                cosine = jnp.broadcast_to(cosines[b, pl.ds(j * slots + k, 1), :], (8, LANES)).astype(BF)
                cosine = jnp.concatenate([cosine] * (channels // 8), axis=0)
                y = p + (q_s[k] + cosine * wc[...])
                tree_push(stack, y + y * jnp.tanh(y))
            angular_out[step, j] = (tree_total(stack).astype(F32) * inverse).astype(BF)
            return inner

        lax.fori_loop(0, slots, slot, 0)
        return carry

    lax.fori_loop(0, steps, block, 0)


def run_angle(layer, start, steps, bonds, counts, cosines, weights, shape):
    first = layer == 0
    per, slots, channels, _ = shape
    sds = jax.ShapeDtypeStruct
    outs = [sds((steps, slots, channels, LANES), BF)]
    scratch = [
        pltpu.VMEM((2 * channels, channels), BF),
        pltpu.VMEM((channels, LANES), BF),
        pltpu.VMEM((slots, channels, LANES), BF),
        pltpu.VMEM((slots, channels, LANES), BF),
    ]
    if first:
        outs += [sds(shape, BF), sds((per, slots * slots, LANES), F32)]
    return pl.pallas_call(
        functools.partial(angle_kernel, layer, first, start, steps, slots, channels),
        out_shape=outs,
        in_specs=[VMEM] * 5,
        out_specs=[VMEM] * len(outs),
        scratch_shapes=scratch,
        compiler_params=PARAMS,
        cost_estimate=pl.CostEstimate(flops=2**30 * steps, bytes_accessed=2**21 * steps, transcendentals=2**22 * steps),
    )(bonds, counts, cosines, *weights)


def update_kernel(layer, slots, channels, parts, *refs):
    angular_refs = refs[:parts]
    bond_ref, gate_ref, wbond_ref, bonds_out, bond_t, done, sems = refs[parts:]
    bond_t[...] = (wbond_ref[layer].astype(F32).T * 0.5).astype(BF)
    copies = []
    b = 0
    for angular_ref in angular_refs:
        for step in range(angular_ref.shape[0]):
            for pair in range(slots // 2):
                both = [
                    bond_update(bond_t[...], angular_ref[step, j], bond_ref[b, j], gate_ref[b, j].astype(F32))
                    for j in (2 * pair, 2 * pair + 1)
                ]
                both = jnp.concatenate(both, axis=0).astype(F32).T.astype(BF)
                done[b, :, pair * 2 * channels : (pair + 1) * 2 * channels] = both
            copies.append(
                pltpu.make_async_copy(done.at[b], bonds_out.at[pl.ds(b * LANES, LANES)], sems.at[b])
            )
            copies[-1].start()
            b += 1
    for copy in copies:
        copy.wait()


def run_update(layer, angulars, bonds, gates, weight):
    per, slots, channels, _ = bonds.shape
    return pl.pallas_call(
        functools.partial(update_kernel, layer, slots, channels, len(angulars)),
        out_shape=jax.ShapeDtypeStruct((per * LANES, slots * channels), BF),
        in_specs=[VMEM] * (len(angulars) + 3),
        out_specs=ANY,
        scratch_shapes=[
            pltpu.VMEM((channels, channels), BF),
            pltpu.VMEM((per, LANES, slots * channels), BF),
            pltpu.SemaphoreType.DMA((per,)),
        ],
        compiler_params=PARAMS,
        cost_estimate=pl.CostEstimate(flops=2**30, bytes_accessed=2**23, transcendentals=0),
    )(*angulars, bonds, gates, weight)


def passed_along(value, steps):
    count = lax.axis_size(AXES)
    return lax.ppermute(value, AXES, [(source, (source + steps) % count) for source in range(count)])


def far_side(domain, quarter):
    rim = 2 * quarter
    rep = lax.axis_size("rep")
    total = lax.axis_size(AXES)
    payload = jnp.where(lax.axis_index("rep") < 2, domain[:, :rim], domain[:, -rim:]).astype(BF)
    pairs = []
    for start in range(0, total, rep):
        for d in range(2):
            pairs.append(((start + d - 2) % total, start + d))
            pairs.append(((start + rep + d) % total, start + rep - 2 + d))
    return lax.ppermute(payload, AXES, pairs)


def sum_stages():
    rep, space = lax.axis_size("rep"), lax.axis_size("space")

    def over_rep(value):
        moved = [
            lax.ppermute(value, "rep", [(i, (i + s) % rep) for i in range(rep)]) for s in range(1, rep)
        ]
        return sum(moved, value)

    def over_space(step):
        return lambda value: value + lax.ppermute(value, "space", [(i, i ^ step) for i in range(space)])

    return [over_rep] + [over_space(1 << s) for s in range(space.bit_length() - 1)]


def per_device(
    atom_features,
    bond_features,
    offsets,
    counts,
    cosines,
    weight_core,
    weight_atom,
    weight_pair,
    weight_cosine,
    weight_bond,
    weight_energy,
):
    quarter = offsets.shape[0]
    per = quarter // LANES
    domain = atom_features.T
    offs = offsets.T
    cnts = counts[None, :]
    into_atoms = (weight_core, weight_atom)
    into_angles = (weight_pair, weight_cosine)
    shape = (per, offsets.shape[1], domain.shape[0], LANES)
    far = far_side(domain, quarter)
    angular, bonds, tiles = run_angle(0, 0, per, bond_features, cnts, cosines, into_angles, shape)
    state, table, bonds = run_gather(
        0, [domain, far], None, bonds, offs, cnts, into_atoms, [angular, weight_bond]
    )
    pieces = [table if s == 0 else passed_along(table, s) for s in (2, 1, 0, -1, -2)]
    half = per // 2
    angulars = list(run_angle(1, 0, half, bonds, cnts, tiles, into_angles, shape))
    state, gates, energy = run_gather(
        1, pieces, state, bonds, offs, cnts, into_atoms, [weight_energy[None, :], angulars[0]]
    )
    stages = sum_stages()
    for part in range(half, per):
        if stages:
            energy = stages.pop(0)(energy)
        angulars += run_angle(1, part, 1, bonds, cnts, tiles, into_angles, shape)
    if stages:
        energy = stages.pop(0)(energy)
    out = run_update(1, angulars, bonds, gates, weight_bond)
    for stage in stages:
        energy = stage(energy)
    scale = math.sqrt(lax.axis_size("space") * domain.shape[1])
    return (state.T, out, jnp.sum(energy) / scale)


def solution(mesh):
    return jax.shard_map(
        per_device,
        mesh=mesh,
        in_specs=(
            P("space", None),
            P(("space", "rep"), None),
            P(("space", "rep"), None),
            P(("space", "rep")),
            P(("space", "rep"), None),
            P(),
            P(),
            P(),
            P(),
            P(),
            P(),
        ),
        out_specs=(P(("space", "rep"), None), P(("space", "rep"), None), P()),
        check_vma=False,
    )
```

```python
import functools
import math

import jax
import jax.numpy as jnp
from jax import lax
from jax.experimental import pallas as pl
from jax.experimental.pallas import tpu as pltpu
from jax.sharding import PartitionSpec as P

LAYERS = 2
LANES = 256
DEAD = -1e30
BATCH = 4
BF = jnp.bfloat16
F32 = jnp.float32
AXES = ("space", "rep")
PARAMS = pltpu.CompilerParams(vmem_limit_bytes=24 * 2**20)
VMEM = pl.BlockSpec(memory_space=pltpu.VMEM)
ANY = pl.BlockSpec(memory_space=pl.ANY)


def tree_push(stack, term):
    level = 0
    while stack and stack[-1][0] == level:
        term = term + stack.pop()[1]
        level += 1
    stack.append((level, term))


def tree_total(stack):
    total = stack.pop()[1]
    while stack:
        total = total + stack.pop()[1]
    return total


def bond_update(weight, angular, bond, gate):
    change = jnp.dot(weight, angular, preferred_element_type=F32)
    return (bond.astype(F32) + change * gate).astype(BF)


def block_lanes(b):
    return pl.ds(pl.multiple_of(b * LANES, LANES), LANES)


def gather_kernel(layer, first, last, slots, channels, quarter, *refs):
    refs = list(refs)
    per = quarter // LANES
    rim = 2 * per
    reach = 2 * rim + 1
    if first:
        state_ref, far_ref = refs[:2]
        refs = refs[2:]
    else:
        piece_refs = refs[:5]
        state_ref = refs[5]
        refs = refs[6:]
    bond_ref, off_ref, cnt_ref, core_ref, atom_ref = refs[:5]
    refs = refs[5:]
    if last:
        energy_w_ref = refs.pop(0)
        refs.pop(0)
    else:
        angular_ref, wbond_ref = refs[:2]
        refs = refs[2:]
    state_out = refs.pop(0)
    if last:
        gate_out, energy_out = refs[:2]
        energy_out[...] = jnp.zeros_like(energy_out)
        energy_w = energy_w_ref[...].T
    else:
        table_out, bonds_out = refs[:2]
    refs = refs[2:]
    tab, core_t, atom_t, bond_t, n_s, msg_s = refs
    core_t[...] = (core_ref[layer].astype(F32).T * 0.5).astype(BF)
    atom_t[...] = atom_ref[layer].astype(F32).T.astype(BF)
    if not last:
        bond_t[...] = (wbond_ref[layer].astype(F32).T * 0.5).astype(BF)
    skip = lax.axis_index("rep") * per if first else 0
    if first:
        inner = state_ref.shape[1] // LANES
        for i in range(inner):
            tab[rim + i] = state_ref[:, i * LANES : (i + 1) * LANES].astype(BF)
        for i in range(rim):
            part = far_ref[:, i * LANES : (i + 1) * LANES]
            tab[i] = part
            tab[rim + inner + i] = part
    else:
        for piece, ref in enumerate(piece_refs):
            for i in range(per):
                tab[piece * per + i] = ref[:, i * LANES : (i + 1) * LANES]
    columns = lax.broadcasted_iota(jnp.int32, (LANES, LANES), 0)
    lane = lax.broadcasted_iota(jnp.int32, (1, LANES), 1) + rim * LANES

    def block(b, carry):
        base = skip + b
        here = block_lanes(b)
        own = tab[base + rim]
        count = cnt_ref[:, here]

        def gather(group):
            for j in range(group * BATCH, (group + 1) * BATCH):
                index = off_ref[j : j + 1, here] + lane
                low = index % LANES
                high = index // LANES
                chosen = jnp.where(columns == low, 1.0, 0.0).astype(BF)
                lhs = tab[pl.ds(base, reach)].reshape(reach * channels, LANES)
                picked = jnp.dot(lhs, chosen, preferred_element_type=F32)
                result = picked[:channels]
                for h in range(1, reach):
                    result = jnp.where(high == h, picked[h * channels : (h + 1) * channels], result)
                n_s[j] = result.astype(BF)

        def gates(group):
            total = msg_s[...] if group else None
            for u in range(BATCH):
                j = group * BATCH + u
                live = jnp.where(j < count, 1.0, 0.0)
                bond = bond_ref[b, j]
                joined = jnp.concatenate([own, n_s[j], bond], axis=0)
                mixed = jnp.dot(core_t[...], joined, preferred_element_type=F32)
                gate = jnp.tanh(mixed)
                cores = mixed[channels : 2 * channels]
                message = (1.0 + gate[:channels]) * (cores + cores * gate[channels : 2 * channels]) * live
                total = message if total is None else total + message
                bond_gate = (1.0 + gate[2 * channels :]) * live
                if last:
                    gate_out[b, j] = bond_gate.astype(BF)
                else:
                    bonds_out[b, j] = bond_update(bond_t[...], angular_ref[b, j], bond, bond_gate)
            msg_s[...] = total

        groups = slots // BATCH
        gather(0)
        for group in range(1, groups):
            gather(group)
            gates(group - 1)
        gates(groups - 1)
        summed = (msg_s[...] * (0.5 / count.astype(F32))).astype(BF)
        state = state_ref[:, block_lanes(base) if first else here]
        state = state + jnp.dot(atom_t[...], summed, preferred_element_type=F32)
        state_out[:, here] = state
        if last:
            energy_out[...] += jnp.sum(state * energy_w, axis=0, keepdims=True)
        else:
            table_out[:, here] = state.astype(BF)
        return carry

    lax.fori_loop(0, per, block, 0)


def run_gather(layer, tables, state, bonds, offs, counts, weights, extra):
    first, last = layer == 0, layer == LAYERS - 1
    slots, quarter = offs.shape
    channels = weights[1].shape[1]
    per = quarter // LANES
    sds = jax.ShapeDtypeStruct
    operands = list(tables)
    if not first:
        operands.append(state)
    operands += [bonds, offs, counts, *weights, *extra]
    specs = [VMEM] * len(operands)
    slab = sds((per, slots, channels, LANES), BF)
    if last:
        specs[-1] = ANY
        outs = [sds((channels, quarter), F32), slab, sds((1, LANES), F32)]
    else:
        outs = [sds((channels, quarter), F32), sds((channels, quarter), BF), slab]
    rows = (tables[0].shape[1] // LANES + 4 * per) if first else 5 * per
    return pl.pallas_call(
        functools.partial(gather_kernel, layer, first, last, slots, channels, quarter),
        out_shape=outs,
        in_specs=specs,
        out_specs=[VMEM] * len(outs),
        scratch_shapes=[
            pltpu.VMEM((rows, channels, LANES), BF),
            pltpu.VMEM((3 * channels, 3 * channels), BF),
            pltpu.VMEM((channels, channels), BF),
            pltpu.VMEM((channels, channels), BF),
            pltpu.VMEM((slots, channels, LANES), BF),
            pltpu.VMEM((channels, LANES), F32),
        ],
        compiler_params=PARAMS,
        cost_estimate=pl.CostEstimate(flops=10 * 2**30, bytes_accessed=2**23, transcendentals=2**22),
    )(*operands)


def angle_kernel(layer, first, start, steps, slots, channels, *refs):
    bond_ref, cnt_ref, cos_ref, pair_ref, wcos_ref, angular_out = refs[:6]
    refs = refs[6:]
    if first:
        bonds, cosines, pair_t, wc, p_s, q_s = refs
    else:
        pair_t, wc, p_s, q_s = refs
        bonds, cosines = bond_ref, cos_ref
    pair_t[...] = (pair_ref[layer].astype(F32).T * 0.5).astype(BF)
    wc[...] = jnp.broadcast_to((wcos_ref[layer : layer + 1] * 0.5).T, wc.shape).astype(BF)

    def block(step, carry):
        b = start + step
        count = cnt_ref[:, block_lanes(b)]
        inverse = 1.0 / count.astype(F32)
        if first:
            rows = block_lanes(b)
            cosines[b] = cos_ref[rows, :].T
            for pair in range(slots // 2):
                both = bond_ref[rows, pair * 2 * channels : (pair + 1) * 2 * channels].astype(F32).T.astype(BF)
                bonds[b, 2 * pair] = both[:channels]
                bonds[b, 2 * pair + 1] = both[channels:]

        for k in range(slots):
            both = jnp.dot(pair_t[...], bonds[b, k], preferred_element_type=F32)
            p_s[k] = both[:channels].astype(BF)
            q_s[k] = jnp.where(k < count, both[channels:], DEAD).astype(BF)

        def slot(j, inner):
            p = p_s[j]
            stack = []
            for m in range(1, slots):
                k = (j + m) % slots
                cosine = jnp.broadcast_to(cosines[b, pl.ds(j * slots + k, 1), :], (8, LANES)).astype(BF)
                cosine = jnp.concatenate([cosine] * (channels // 8), axis=0)
                y = p + (q_s[k] + cosine * wc[...])
                tree_push(stack, y + y * jnp.tanh(y))
            angular_out[step, j] = (tree_total(stack).astype(F32) * inverse).astype(BF)
            return inner

        lax.fori_loop(0, slots, slot, 0, unroll=2)
        return carry

    lax.fori_loop(0, steps, block, 0)


def run_angle(layer, start, steps, bonds, counts, cosines, weights, shape):
    first = layer == 0
    per, slots, channels, _ = shape
    sds = jax.ShapeDtypeStruct
    outs = [sds((steps, slots, channels, LANES), BF)]
    scratch = [
        pltpu.VMEM((2 * channels, channels), BF),
        pltpu.VMEM((channels, LANES), BF),
        pltpu.VMEM((slots, channels, LANES), BF),
        pltpu.VMEM((slots, channels, LANES), BF),
    ]
    if first:
        outs += [sds(shape, BF), sds((per, slots * slots, LANES), F32)]
    return pl.pallas_call(
        functools.partial(angle_kernel, layer, first, start, steps, slots, channels),
        out_shape=outs,
        in_specs=[VMEM] * 5,
        out_specs=[VMEM] * len(outs),
        scratch_shapes=scratch,
        compiler_params=PARAMS,
        cost_estimate=pl.CostEstimate(flops=2**30 * steps, bytes_accessed=2**21 * steps, transcendentals=2**22 * steps),
    )(bonds, counts, cosines, *weights)


def update_kernel(layer, slots, channels, parts, *refs):
    angular_refs = refs[:parts]
    bond_ref, gate_ref, wbond_ref, bonds_out, bond_t, done, sems = refs[parts:]
    bond_t[...] = (wbond_ref[layer].astype(F32).T * 0.5).astype(BF)
    copies = []
    b = 0
    for angular_ref in angular_refs:
        for step in range(angular_ref.shape[0]):
            for pair in range(slots // 2):
                both = [
                    bond_update(bond_t[...], angular_ref[step, j], bond_ref[b, j], gate_ref[b, j].astype(F32))
                    for j in (2 * pair, 2 * pair + 1)
                ]
                both = jnp.concatenate(both, axis=0).astype(F32).T.astype(BF)
                done[b, :, pair * 2 * channels : (pair + 1) * 2 * channels] = both
            copies.append(
                pltpu.make_async_copy(done.at[b], bonds_out.at[pl.ds(b * LANES, LANES)], sems.at[b])
            )
            copies[-1].start()
            b += 1
    for copy in copies:
        copy.wait()


def run_update(layer, angulars, bonds, gates, weight):
    per, slots, channels, _ = bonds.shape
    return pl.pallas_call(
        functools.partial(update_kernel, layer, slots, channels, len(angulars)),
        out_shape=jax.ShapeDtypeStruct((per * LANES, slots * channels), BF),
        in_specs=[VMEM] * (len(angulars) + 3),
        out_specs=ANY,
        scratch_shapes=[
            pltpu.VMEM((channels, channels), BF),
            pltpu.VMEM((per, LANES, slots * channels), BF),
            pltpu.SemaphoreType.DMA((per,)),
        ],
        compiler_params=PARAMS,
        cost_estimate=pl.CostEstimate(flops=2**30, bytes_accessed=2**23, transcendentals=0),
    )(*angulars, bonds, gates, weight)


def passed_along(value, steps):
    count = lax.axis_size(AXES)
    return lax.ppermute(value, AXES, [(source, (source + steps) % count) for source in range(count)])


def edge_kernel(domain_ref, payload_ref):
    rim = payload_ref.shape[1]
    start = jnp.where(lax.axis_index("rep") < 2, domain_ref.shape[1] - rim, 0)
    payload_ref[...] = domain_ref[:, pl.ds(pl.multiple_of(start, LANES), rim)].astype(BF)


def far_side(domain, quarter):
    rim = 2 * quarter
    rep = lax.axis_size("rep")
    total = lax.axis_size(AXES)
    payload = pl.pallas_call(
        edge_kernel,
        out_shape=jax.ShapeDtypeStruct((domain.shape[0], rim), BF),
        in_specs=[VMEM],
        out_specs=VMEM,
        compiler_params=PARAMS,
        cost_estimate=pl.CostEstimate(flops=10 * 2**30, bytes_accessed=2**23, transcendentals=2**22),
    )(domain)
    pairs = []
    for start in range(0, total, rep):
        for d in range(rep):
            pairs.append(((start + d + (-rep if d < 2 else rep)) % total, start + d))
    return lax.ppermute(payload, AXES, pairs)


def sum_stages():
    rep, space = lax.axis_size("rep"), lax.axis_size("space")

    def over_rep(value):
        moved = [
            lax.ppermute(value, "rep", [(i, (i + s) % rep) for i in range(rep)]) for s in range(1, rep)
        ]
        return sum(moved, value)

    def over_space(step):
        return lambda value: value + lax.ppermute(value, "space", [(i, i ^ step) for i in range(space)])

    return [over_rep] + [over_space(1 << s) for s in range(space.bit_length() - 1)]


def per_device(
    atom_features,
    bond_features,
    offsets,
    counts,
    cosines,
    weight_core,
    weight_atom,
    weight_pair,
    weight_cosine,
    weight_bond,
    weight_energy,
):
    quarter = offsets.shape[0]
    per = quarter // LANES
    domain = atom_features.T
    offs = offsets.T
    cnts = counts[None, :]
    into_atoms = (weight_core, weight_atom)
    into_angles = (weight_pair, weight_cosine)
    shape = (per, offsets.shape[1], domain.shape[0], LANES)
    far = far_side(domain, quarter)
    angular, bonds, tiles = run_angle(0, 0, per, bond_features, cnts, cosines, into_angles, shape)
    state, table, bonds = run_gather(
        0, [domain, far], None, bonds, offs, cnts, into_atoms, [angular, weight_bond]
    )
    pieces = [table if s == 0 else passed_along(table, s) for s in (2, 1, 0, -1, -2)]
    half = per // 2
    angulars = list(run_angle(1, 0, half, bonds, cnts, tiles, into_angles, shape))
    state, gates, energy = run_gather(
        1, pieces, state, bonds, offs, cnts, into_atoms, [weight_energy[None, :], angulars[0]]
    )
    stages = sum_stages()
    for part in range(half, per):
        if stages:
            energy = stages.pop(0)(energy)
        angulars += run_angle(1, part, 1, bonds, cnts, tiles, into_angles, shape)
    if stages:
        energy = stages.pop(0)(energy)
    out = run_update(1, angulars, bonds, gates, weight_bond)
    for stage in stages:
        energy = stage(energy)
    scale = math.sqrt(lax.axis_size("space") * domain.shape[1])
    return (state.T, out, jnp.sum(energy) / scale)


def solution(mesh):
    return jax.shard_map(
        per_device,
        mesh=mesh,
        in_specs=(
            P("space", None),
            P(("space", "rep"), None),
            P(("space", "rep"), None),
            P(("space", "rep")),
            P(("space", "rep"), None),
            P(),
            P(),
            P(),
            P(),
            P(),
            P(),
        ),
        out_specs=(P(("space", "rep"), None), P(("space", "rep"), None), P()),
        check_vma=False,
    )
```

```python
import functools
import math

import jax
import jax.numpy as jnp
from jax import lax
from jax.experimental import pallas as pl
from jax.experimental.pallas import tpu as pltpu
from jax.sharding import PartitionSpec as P

LAYERS = 2
LANES = 256
DEAD = -1e30
BATCH = 4
BF = jnp.bfloat16
F32 = jnp.float32
AXES = ("space", "rep")
PARAMS = pltpu.CompilerParams(vmem_limit_bytes=24 * 2**20)
VMEM = pl.BlockSpec(memory_space=pltpu.VMEM)
ANY = pl.BlockSpec(memory_space=pl.ANY)


def tree_push(stack, term):
    level = 0
    while stack and stack[-1][0] == level:
        term = term + stack.pop()[1]
        level += 1
    stack.append((level, term))


def tree_total(stack):
    total = stack.pop()[1]
    while stack:
        total = total + stack.pop()[1]
    return total


def bond_update(weight, angular, bond, gate):
    change = jnp.dot(weight, angular, preferred_element_type=F32)
    return (bond.astype(F32) + change * gate).astype(BF)


def block_lanes(b):
    return pl.ds(pl.multiple_of(b * LANES, LANES), LANES)


def gather_kernel(layer, first, last, slots, channels, quarter, *refs):
    refs = list(refs)
    per = quarter // LANES
    rim = 2 * per
    reach = 2 * rim + 1
    if first:
        state_ref, far_ref = refs[:2]
        refs = refs[2:]
    else:
        piece_refs = refs[:5]
        state_ref = refs[5]
        refs = refs[6:]
    bond_ref, off_ref, cnt_ref, core_ref, atom_ref = refs[:5]
    refs = refs[5:]
    if last:
        energy_w_ref = refs.pop(0)
        refs.pop(0)
    else:
        angular_ref, wbond_ref = refs[:2]
        refs = refs[2:]
    state_out = refs.pop(0)
    if last:
        gate_out, energy_out = refs[:2]
        energy_out[...] = jnp.zeros_like(energy_out)
        energy_w = energy_w_ref[...].T
    else:
        table_out, bonds_out = refs[:2]
    refs = refs[2:]
    tab, core_t, atom_t, bond_t, n_s, msg_s = refs
    core_t[...] = (core_ref[layer].astype(F32).T * 0.5).astype(BF)
    atom_t[...] = atom_ref[layer].astype(F32).T.astype(BF)
    if not last:
        bond_t[...] = (wbond_ref[layer].astype(F32).T * 0.5).astype(BF)
    skip = lax.axis_index("rep") * per if first else 0
    if first:
        inner = state_ref.shape[1] // LANES
        for i in range(inner):
            tab[rim + i] = state_ref[:, i * LANES : (i + 1) * LANES].astype(BF)
        for i in range(rim):
            part = far_ref[:, i * LANES : (i + 1) * LANES]
            tab[i] = part
            tab[rim + inner + i] = part
    else:
        for piece, ref in enumerate(piece_refs):
            for i in range(per):
                tab[piece * per + i] = ref[:, i * LANES : (i + 1) * LANES]
    columns = lax.broadcasted_iota(jnp.int32, (LANES, LANES), 0)
    lane = lax.broadcasted_iota(jnp.int32, (1, LANES), 1) + rim * LANES

    def gather(b, group):
        base = skip + b
        here = slice(b * LANES, (b + 1) * LANES)
        for u in range(BATCH):
            j = group * BATCH + u
            index = off_ref[j : j + 1, here] + lane
            low = index % LANES
            high = index // LANES
            chosen = jnp.where(columns == low, 1.0, 0.0).astype(BF)
            lhs = tab[pl.ds(base, reach)].reshape(reach * channels, LANES)
            picked = jnp.dot(lhs, chosen, preferred_element_type=F32)
            result = picked[:channels]
            for h in range(1, reach):
                result = jnp.where(high == h, picked[h * channels : (h + 1) * channels], result)
            n_s[group % 2, u] = result.astype(BF)

    def gates(b, group):
        base = skip + b
        here = slice(b * LANES, (b + 1) * LANES)
        own = tab[base + rim]
        count = cnt_ref[:, here]
        total = msg_s[...] if group else None
        for u in range(BATCH):
            j = group * BATCH + u
            live = jnp.where(j < count, 1.0, 0.0)
            bond = bond_ref[b, j]
            joined = jnp.concatenate([own, n_s[group % 2, u], bond], axis=0)
            mixed = jnp.dot(core_t[...], joined, preferred_element_type=F32)
            gate = jnp.tanh(mixed)
            cores = mixed[channels : 2 * channels]
            message = (1.0 + gate[:channels]) * (cores + cores * gate[channels : 2 * channels]) * live
            total = message if total is None else total + message
            bond_gate = (1.0 + gate[2 * channels :]) * live
            if last:
                gate_out[b, j] = bond_gate.astype(BF)
            else:
                bonds_out[b, j] = bond_update(bond_t[...], angular_ref[b, j], bond, bond_gate)
        if group < slots // BATCH - 1:
            msg_s[...] = total
            return
        summed = (total * (0.5 / count.astype(F32))).astype(BF)
        state = state_ref[:, block_lanes(base) if first else here]
        state = state + jnp.dot(atom_t[...], summed, preferred_element_type=F32)
        state_out[:, here] = state
        if last:
            energy_out[...] += jnp.sum(state * energy_w, axis=0, keepdims=True)
        else:
            table_out[:, here] = state.astype(BF)

    work = [(b, group) for b in range(per) for group in range(slots // BATCH)]
    gather(*work[0])
    for now, before in zip(work[1:], work[:-1]):
        gather(*now)
        gates(*before)
    gates(*work[-1])


def run_gather(layer, tables, state, bonds, offs, counts, weights, extra):
    first, last = layer == 0, layer == LAYERS - 1
    slots, quarter = offs.shape
    channels = weights[1].shape[1]
    per = quarter // LANES
    sds = jax.ShapeDtypeStruct
    operands = list(tables)
    if not first:
        operands.append(state)
    operands += [bonds, offs, counts, *weights, *extra]
    specs = [VMEM] * len(operands)
    slab = sds((per, slots, channels, LANES), BF)
    if last:
        specs[-1] = ANY
        outs = [sds((channels, quarter), F32), slab, sds((1, LANES), F32)]
    else:
        outs = [sds((channels, quarter), F32), sds((channels, quarter), BF), slab]
    rows = (tables[0].shape[1] // LANES + 4 * per) if first else 5 * per
    return pl.pallas_call(
        functools.partial(gather_kernel, layer, first, last, slots, channels, quarter),
        out_shape=outs,
        in_specs=specs,
        out_specs=[VMEM] * len(outs),
        scratch_shapes=[
            pltpu.VMEM((rows, channels, LANES), BF),
            pltpu.VMEM((3 * channels, 3 * channels), BF),
            pltpu.VMEM((channels, channels), BF),
            pltpu.VMEM((channels, channels), BF),
            pltpu.VMEM((2, BATCH, channels, LANES), BF),
            pltpu.VMEM((channels, LANES), F32),
        ],
        compiler_params=PARAMS,
        cost_estimate=pl.CostEstimate(flops=10 * 2**30, bytes_accessed=2**23, transcendentals=2**22),
    )(*operands)


def angle_kernel(layer, first, start, steps, slots, channels, *refs):
    bond_ref, cnt_ref, cos_ref, pair_ref, wcos_ref, angular_out = refs[:6]
    refs = refs[6:]
    if first:
        bonds, cosines, pair_t, wc, p_s, q_s = refs
    else:
        pair_t, wc, p_s, q_s = refs
        bonds, cosines = bond_ref, cos_ref
    pair_t[...] = (pair_ref[layer].astype(F32).T * 0.5).astype(BF)
    wc[...] = jnp.broadcast_to((wcos_ref[layer : layer + 1] * 0.5).T, wc.shape).astype(BF)

    def block(step, carry):
        b = start + step
        count = cnt_ref[:, block_lanes(b)]
        inverse = 1.0 / count.astype(F32)
        if first:
            rows = block_lanes(b)
            cosines[b] = cos_ref[rows, :].T
            for pair in range(slots // 2):
                both = bond_ref[rows, pair * 2 * channels : (pair + 1) * 2 * channels].astype(F32).T.astype(BF)
                bonds[b, 2 * pair] = both[:channels]
                bonds[b, 2 * pair + 1] = both[channels:]

        for k in range(slots):
            both = jnp.dot(pair_t[...], bonds[b, k], preferred_element_type=F32)
            p_s[k] = both[:channels].astype(BF)
            q_s[k] = jnp.where(k < count, both[channels:], DEAD).astype(BF)

        def slot(j, inner):
            p = p_s[j]
            stack = []
            for m in range(1, slots):
                k = (j + m) % slots
                cosine = jnp.broadcast_to(cosines[b, pl.ds(j * slots + k, 1), :], (8, LANES)).astype(BF)
                cosine = jnp.concatenate([cosine] * (channels // 8), axis=0)
                y = p + (q_s[k] + cosine * wc[...])
                tree_push(stack, y + y * jnp.tanh(y))
            angular_out[step, j] = (tree_total(stack).astype(F32) * inverse).astype(BF)
            return inner

        lax.fori_loop(0, slots, slot, 0, unroll=2)
        return carry

    lax.fori_loop(0, steps, block, 0)


def run_angle(layer, start, steps, bonds, counts, cosines, weights, shape):
    first = layer == 0
    per, slots, channels, _ = shape
    sds = jax.ShapeDtypeStruct
    outs = [sds((steps, slots, channels, LANES), BF)]
    scratch = [
        pltpu.VMEM((2 * channels, channels), BF),
        pltpu.VMEM((channels, LANES), BF),
        pltpu.VMEM((slots, channels, LANES), BF),
        pltpu.VMEM((slots, channels, LANES), BF),
    ]
    if first:
        outs += [sds(shape, BF), sds((per, slots * slots, LANES), F32)]
    return pl.pallas_call(
        functools.partial(angle_kernel, layer, first, start, steps, slots, channels),
        out_shape=outs,
        in_specs=[VMEM] * 5,
        out_specs=[VMEM] * len(outs),
        scratch_shapes=scratch,
        compiler_params=PARAMS,
        cost_estimate=pl.CostEstimate(flops=2**30 * steps, bytes_accessed=2**21 * steps, transcendentals=2**22 * steps),
    )(bonds, counts, cosines, *weights)


def update_kernel(layer, start, slots, channels, parts, *refs):
    angular_refs = refs[:parts]
    bond_ref, gate_ref, wbond_ref, _, bonds_out, bond_t, done, sems = refs[parts:]
    bond_t[...] = (wbond_ref[layer].astype(F32).T * 0.5).astype(BF)
    copies = []
    b = start
    for angular_ref in angular_refs:
        for step in range(angular_ref.shape[0]):
            for pair in range(slots // 2):
                both = [
                    bond_update(bond_t[...], angular_ref[step, j], bond_ref[b, j], gate_ref[b, j].astype(F32))
                    for j in (2 * pair, 2 * pair + 1)
                ]
                both = jnp.concatenate(both, axis=0).astype(F32).T.astype(BF)
                done[b - start, :, pair * 2 * channels : (pair + 1) * 2 * channels] = both
            copies.append(
                pltpu.make_async_copy(done.at[b - start], bonds_out.at[pl.ds(b * LANES, LANES)], sems.at[b - start])
            )
            copies[-1].start()
            b += 1
    for copy in copies:
        copy.wait()


def run_update(layer, start, buffer, angulars, bonds, gates, weight):
    per, slots, channels, _ = bonds.shape
    parts = len(angulars)
    return pl.pallas_call(
        functools.partial(update_kernel, layer, start, slots, channels, parts),
        out_shape=jax.ShapeDtypeStruct((per * LANES, slots * channels), BF),
        in_specs=[VMEM] * (parts + 3) + [ANY],
        out_specs=ANY,
        input_output_aliases={} if buffer is None else {parts + 3: 0},
        scratch_shapes=[
            pltpu.VMEM((channels, channels), BF),
            pltpu.VMEM((per, LANES, slots * channels), BF),
            pltpu.SemaphoreType.DMA((per,)),
        ],
        compiler_params=PARAMS,
        cost_estimate=pl.CostEstimate(flops=2**30, bytes_accessed=2**23, transcendentals=0),
    )(*angulars, bonds, gates, weight, weight if buffer is None else buffer)


def passed_along(value, steps):
    count = lax.axis_size(AXES)
    return lax.ppermute(value, AXES, [(source, (source + steps) % count) for source in range(count)])


def edge_kernel(domain_ref, payload_ref):
    rim = payload_ref.shape[1]
    start = jnp.where(lax.axis_index("rep") < 2, domain_ref.shape[1] - rim, 0)
    payload_ref[...] = domain_ref[:, pl.ds(pl.multiple_of(start, LANES), rim)].astype(BF)


def far_side(domain, quarter):
    rim = 2 * quarter
    rep = lax.axis_size("rep")
    total = lax.axis_size(AXES)
    payload = pl.pallas_call(
        edge_kernel,
        out_shape=jax.ShapeDtypeStruct((domain.shape[0], rim), BF),
        in_specs=[VMEM],
        out_specs=VMEM,
        compiler_params=PARAMS,
        cost_estimate=pl.CostEstimate(flops=10 * 2**30, bytes_accessed=2**23, transcendentals=2**22),
    )(domain)
    pairs = []
    for start in range(0, total, rep):
        for d in range(rep):
            pairs.append(((start + d + (-rep if d < 2 else rep)) % total, start + d))
    return lax.ppermute(payload, AXES, pairs)


def sum_stages():
    def exchange(axis, step):
        size = lax.axis_size(axis)
        return lambda value: value + lax.ppermute(value, axis, [(i, i ^ step) for i in range(size)])

    return [
        exchange(axis, 1 << bit)
        for axis in ("rep", "space")
        for bit in range(lax.axis_size(axis).bit_length() - 1)
    ]


def per_device(
    atom_features,
    bond_features,
    offsets,
    counts,
    cosines,
    weight_core,
    weight_atom,
    weight_pair,
    weight_cosine,
    weight_bond,
    weight_energy,
):
    quarter = offsets.shape[0]
    per = quarter // LANES
    domain = atom_features.T
    offs = offsets.T
    cnts = counts[None, :]
    into_atoms = (weight_core, weight_atom)
    into_angles = (weight_pair, weight_cosine)
    shape = (per, offsets.shape[1], domain.shape[0], LANES)
    far = far_side(domain, quarter)
    angular, bonds, tiles = run_angle(0, 0, per, bond_features, cnts, cosines, into_angles, shape)
    state, table, bonds = run_gather(
        0, [domain, far], None, bonds, offs, cnts, into_atoms, [angular, weight_bond]
    )
    pieces = [table if s == 0 else passed_along(table, s) for s in (2, 1, 0, -1, -2)]
    half = per // 2
    angulars = list(run_angle(1, 0, half, bonds, cnts, tiles, into_angles, shape))
    state, gates, energy = run_gather(
        1, pieces, state, bonds, offs, cnts, into_atoms, [weight_energy[None, :], angulars[0]]
    )
    stages = sum_stages()
    for part in range(half, per):
        if stages:
            energy = stages.pop(0)(energy)
        angulars += run_angle(1, part, 1, bonds, cnts, tiles, into_angles, shape)
    out = None
    for part in range(2):
        if stages:
            energy = stages.pop(0)(energy)
        mine = angulars[:1] if part == 0 else angulars[1:]
        out = run_update(1, part * half, out, mine, bonds, gates, weight_bond)
    for stage in stages:
        energy = stage(energy)
    scale = math.sqrt(lax.axis_size("space") * domain.shape[1])
    return (state.T, out, jnp.sum(energy) / scale)


def solution(mesh):
    return jax.shard_map(
        per_device,
        mesh=mesh,
        in_specs=(
            P("space", None),
            P(("space", "rep"), None),
            P(("space", "rep"), None),
            P(("space", "rep")),
            P(("space", "rep"), None),
            P(),
            P(),
            P(),
            P(),
            P(),
            P(),
        ),
        out_specs=(P(("space", "rep"), None), P(("space", "rep"), None), P()),
        check_vma=False,
    )
```

```python
import functools
import math

import jax
import jax.numpy as jnp
from jax import lax
from jax.experimental import pallas as pl
from jax.experimental.pallas import tpu as pltpu
from jax.sharding import PartitionSpec as P

LAYERS = 2
LANES = 256
DEAD = -1e30
BATCH = 4
EARLY = 3
HIDING = 2
BF = jnp.bfloat16
F32 = jnp.float32
AXES = ("space", "rep")
PARAMS = pltpu.CompilerParams(vmem_limit_bytes=24 * 2**20)
VMEM = pl.BlockSpec(memory_space=pltpu.VMEM)
ANY = pl.BlockSpec(memory_space=pl.ANY)


def tree_push(stack, term):
    level = 0
    while stack and stack[-1][0] == level:
        term = term + stack.pop()[1]
        level += 1
    stack.append((level, term))


def tree_total(stack):
    total = stack.pop()[1]
    while stack:
        total = total + stack.pop()[1]
    return total


def bond_update(weight, angular, bond, gate):
    change = jnp.dot(weight, angular, preferred_element_type=F32)
    return (bond.astype(F32) + change * gate).astype(BF)


def project(pair_t, bond, live):
    channels = bond.shape[0]
    both = jnp.dot(pair_t, bond, preferred_element_type=F32)
    return both[:channels].astype(BF), jnp.where(live, both[channels:], DEAD).astype(BF)


def angle_sum(p, queries, cosine_row, wc, j, slots, inverse):
    stack = []
    for m in range(1, slots):
        k = (j + m) % slots
        cosine = jnp.broadcast_to(cosine_row(k), (8, LANES)).astype(BF)
        cosine = jnp.concatenate([cosine] * (p.shape[0] // 8), axis=0)
        y = p + (queries(k) + cosine * wc[...])
        tree_push(stack, y + y * jnp.tanh(y))
    return (tree_total(stack).astype(F32) * inverse).astype(BF)


def block_lanes(b):
    return pl.ds(pl.multiple_of(b * LANES, LANES), LANES)


def gather_kernel(layer, first, last, slots, channels, quarter, *refs):
    refs = list(refs)
    per = quarter // LANES
    rim = 2 * per
    reach = 2 * rim + 1
    if first:
        state_ref, far_ref = refs[:2]
        refs = refs[2:]
    else:
        piece_refs = refs[:5]
        state_ref = refs[5]
        refs = refs[6:]
    bond_ref, off_ref, cnt_ref, core_ref, atom_ref = refs[:5]
    refs = refs[5:]
    if last:
        energy_w_ref = refs.pop(0)
        refs.pop(0)
    else:
        wcos_ref, cos_ref, p_ref, q_ref = refs[:4]
        refs = refs[4:]
        early = bond_ref.shape[0] - p_ref.shape[0]
    state_out, gate_out, third_out = refs[:3]
    refs = refs[3:]
    if not last:
        late = refs.pop(0)
    if last:
        energy_out = third_out
        energy_out[...] = jnp.zeros_like(energy_out)
        energy_w = energy_w_ref[...].T
    tab, core_t, atom_t, n_s, msg_s, wc = refs
    core_t[...] = (core_ref[layer].astype(F32).T * 0.5).astype(BF)
    atom_t[...] = atom_ref[layer].astype(F32).T.astype(BF)
    if not last:
        wc[...] = jnp.broadcast_to((wcos_ref[layer : layer + 1] * 0.5).T, wc.shape).astype(BF)
    skip = lax.axis_index("rep") * per if first else 0
    if first:
        inner = state_ref.shape[1] // LANES
        for i in range(inner):
            tab[rim + i] = state_ref[:, i * LANES : (i + 1) * LANES].astype(BF)
        for i in range(rim):
            part = far_ref[:, i * LANES : (i + 1) * LANES]
            tab[i] = part
            tab[rim + inner + i] = part
    else:
        for piece, ref in enumerate(piece_refs):
            for i in range(per):
                tab[piece * per + i] = ref[:, i * LANES : (i + 1) * LANES]
    columns = lax.broadcasted_iota(jnp.int32, (LANES, LANES), 0)
    lane = lax.broadcasted_iota(jnp.int32, (1, LANES), 1) + rim * LANES

    def late_angle(b, j):
        inverse = 1.0 / cnt_ref[:, b * LANES : (b + 1) * LANES].astype(F32)
        step = b - early
        late[step, j] = angle_sum(
            p_ref[step, j],
            lambda k: q_ref[step, k],
            lambda k: cos_ref[b, j * slots + k : j * slots + k + 1, :],
            wc,
            j,
            slots,
            inverse,
        )

    def gather(b, group, rows):
        base = skip + b
        here = slice(b * LANES, (b + 1) * LANES)
        for u in range(BATCH):
            j = group * BATCH + u
            index = off_ref[j : j + 1, here] + lane
            low = index % LANES
            high = index // LANES
            chosen = jnp.where(columns == low, 1.0, 0.0).astype(BF)
            lhs = tab[pl.ds(base, reach)].reshape(reach * channels, LANES)
            picked = jnp.dot(lhs, chosen, preferred_element_type=F32)
            result = picked[:channels]
            for h in range(1, reach):
                result = jnp.where(high == h, picked[h * channels : (h + 1) * channels], result)
            n_s[group % 2, u] = result.astype(BF)
            for row in rows[u * len(rows) // BATCH : (u + 1) * len(rows) // BATCH]:
                late_angle(*row)

    def gates(b, group):
        base = skip + b
        here = slice(b * LANES, (b + 1) * LANES)
        own = tab[base + rim]
        count = cnt_ref[:, here]
        total = msg_s[...] if group else None
        for u in range(BATCH):
            j = group * BATCH + u
            live = jnp.where(j < count, 1.0, 0.0)
            bond = bond_ref[b, j]
            joined = jnp.concatenate([own, n_s[group % 2, u], bond], axis=0)
            mixed = jnp.dot(core_t[...], joined, preferred_element_type=F32)
            gate = jnp.tanh(mixed)
            cores = mixed[channels : 2 * channels]
            message = (1.0 + gate[:channels]) * (cores + cores * gate[channels : 2 * channels]) * live
            total = message if total is None else total + message
            bond_gate = (1.0 + gate[2 * channels :]) * live
            gate_out[b, j] = bond_gate.astype(BF)
        if group < slots // BATCH - 1:
            msg_s[...] = total
            return
        summed = (total * (0.5 / count.astype(F32))).astype(BF)
        state = state_ref[:, block_lanes(base) if first else here]
        state = state + jnp.dot(atom_t[...], summed, preferred_element_type=F32)
        state_out[:, here] = state
        if last:
            energy_out[...] += jnp.sum(state * energy_w, axis=0, keepdims=True)
        else:
            third_out[:, here] = state.astype(BF)

    work = [(b, group) for b in range(per) for group in range(slots // BATCH)]
    rows = [] if last else [(b, j) for b in range(early, per) for j in range(slots)]
    share = len(rows) // len(work)
    gather(*work[0], rows[:share])
    for at in range(1, len(work)):
        gather(*work[at], rows[at * share : (at + 1) * share])
        gates(*work[at - 1])
    gates(*work[-1])


def run_gather(layer, tables, state, bonds, offs, counts, weights, extra):
    first, last = layer == 0, layer == LAYERS - 1
    slots, quarter = offs.shape
    channels = weights[1].shape[1]
    per = quarter // LANES
    sds = jax.ShapeDtypeStruct
    operands = list(tables)
    if not first:
        operands.append(state)
    operands += [bonds, offs, counts, *weights, *extra]
    specs = [VMEM] * len(operands)
    slab = sds((per, slots, channels, LANES), BF)
    if last:
        specs[-1] = ANY
        outs = [sds((channels, quarter), F32), slab, sds((1, LANES), F32)]
    else:
        outs = [sds((channels, quarter), F32), slab, sds((channels, quarter), BF), sds(extra[-1].shape, BF)]
    rows = (tables[0].shape[1] // LANES + 4 * per) if first else 5 * per
    return pl.pallas_call(
        functools.partial(gather_kernel, layer, first, last, slots, channels, quarter),
        out_shape=outs,
        in_specs=specs,
        out_specs=[VMEM] * len(outs),
        scratch_shapes=[
            pltpu.VMEM((rows, channels, LANES), BF),
            pltpu.VMEM((3 * channels, 3 * channels), BF),
            pltpu.VMEM((channels, channels), BF),
            pltpu.VMEM((2, BATCH, channels, LANES), BF),
            pltpu.VMEM((channels, LANES), F32),
            pltpu.VMEM((channels, LANES), BF),
        ],
        compiler_params=PARAMS,
        cost_estimate=pl.CostEstimate(flops=10 * 2**30, bytes_accessed=2**23, transcendentals=2**22),
    )(*operands)


def angle_kernel(layer, first, start, steps, slots, channels, waits, *refs):
    bond_ref, cnt_ref, cos_ref, pair_ref, wcos_ref = refs[:5]
    angular_out = refs[5 + waits]
    refs = refs[6 + waits :]
    if first:
        bonds, cosines, p_out, q_out, pair_t, wc, p_s, q_s = refs
    else:
        pair_t, wc, p_s, q_s = refs
        bonds, cosines = bond_ref, cos_ref
    pair_t[...] = (pair_ref[layer].astype(F32).T * 0.5).astype(BF)
    wc[...] = jnp.broadcast_to((wcos_ref[layer : layer + 1] * 0.5).T, wc.shape).astype(BF)

    def turn(b):
        rows = block_lanes(b)
        cosines[b] = cos_ref[rows, :].T
        for pair in range(slots // 2):
            both = bond_ref[rows, pair * 2 * channels : (pair + 1) * 2 * channels].astype(F32).T.astype(BF)
            bonds[b, 2 * pair] = both[:channels]
            bonds[b, 2 * pair + 1] = both[channels:]

    def block(step, carry):
        b = start + step
        count = cnt_ref[:, block_lanes(b)]
        inverse = 1.0 / count.astype(F32)
        if first:
            turn(b)

        for k in range(slots):
            p_s[k], q_s[k] = project(pair_t[...], bonds[b, k], k < count)

        def slot(j, inner):
            angular_out[step, j] = angle_sum(
                p_s[j],
                lambda k: q_s[k],
                lambda k: cosines[b, pl.ds(j * slots + k, 1), :],
                wc,
                j,
                slots,
                inverse,
            )
            return inner

        lax.fori_loop(0, slots, slot, 0, unroll=2)
        return carry

    lax.fori_loop(0, steps, block, 0)
    if first:

        def later(step, carry):
            b = steps + step
            turn(b)
            count = cnt_ref[:, block_lanes(b)]
            for k in range(slots):
                p_out[step, k], q_out[step, k] = project(pair_t[...], bonds[b, k], k < count)
            return carry

        lax.fori_loop(0, p_out.shape[0], later, 0)


def run_angle(layer, first, start, steps, bonds, counts, cosines, weights, shape, after=()):
    per, slots, channels, _ = shape
    sds = jax.ShapeDtypeStruct
    outs = [sds((steps, slots, channels, LANES), BF)]
    scratch = [
        pltpu.VMEM((2 * channels, channels), BF),
        pltpu.VMEM((channels, LANES), BF),
        pltpu.VMEM((slots, channels, LANES), BF),
        pltpu.VMEM((slots, channels, LANES), BF),
    ]
    if first:
        later = sds((per - steps, slots, channels, LANES), BF)
        outs += [sds(shape, BF), sds((per, slots * slots, LANES), F32), later, later]
    return pl.pallas_call(
        functools.partial(angle_kernel, layer, first, start, steps, slots, channels, len(after)),
        out_shape=outs,
        in_specs=[VMEM] * 5 + [ANY] * len(after),
        out_specs=[VMEM] * len(outs),
        scratch_shapes=scratch,
        compiler_params=PARAMS,
        cost_estimate=pl.CostEstimate(flops=2**30 * steps, bytes_accessed=2**21 * steps, transcendentals=2**22 * steps),
    )(bonds, counts, cosines, *weights, *after)


def inner_update_kernel(layer, slots, parts, *refs):
    bond_ref, gate_ref, wbond_ref, bonds_out, bond_t = refs[parts:]
    bond_t[...] = (wbond_ref[layer].astype(F32).T * 0.5).astype(BF)
    b = 0
    for angular_ref in refs[:parts]:
        for step in range(angular_ref.shape[0]):
            for j in range(slots):
                bonds_out[b, j] = bond_update(
                    bond_t[...], angular_ref[step, j], bond_ref[b, j], gate_ref[b, j].astype(F32)
                )
            b += 1


def run_inner_update(layer, angulars, bonds, gates, weight):
    channels = bonds.shape[2]
    parts = len(angulars)
    return pl.pallas_call(
        functools.partial(inner_update_kernel, layer, bonds.shape[1], parts),
        out_shape=jax.ShapeDtypeStruct(bonds.shape, BF),
        in_specs=[VMEM] * (parts + 3),
        out_specs=VMEM,
        scratch_shapes=[pltpu.VMEM((channels, channels), BF)],
        compiler_params=PARAMS,
        cost_estimate=pl.CostEstimate(flops=2**30, bytes_accessed=2**23, transcendentals=0),
    )(*angulars, bonds, gates, weight)


def update_kernel(layer, start, slots, channels, parts, *refs):
    angular_refs = refs[:parts]
    bond_ref, gate_ref, wbond_ref, _, bonds_out, bond_t, done, sems = refs[parts:]
    bond_t[...] = (wbond_ref[layer].astype(F32).T * 0.5).astype(BF)
    copies = []
    b = start
    for angular_ref in angular_refs:
        for step in range(angular_ref.shape[0]):
            for pair in range(slots // 2):
                both = [
                    bond_update(bond_t[...], angular_ref[step, j], bond_ref[b, j], gate_ref[b, j].astype(F32))
                    for j in (2 * pair, 2 * pair + 1)
                ]
                both = jnp.concatenate(both, axis=0).astype(F32).T.astype(BF)
                done[b - start, :, pair * 2 * channels : (pair + 1) * 2 * channels] = both
            copies.append(
                pltpu.make_async_copy(done.at[b - start], bonds_out.at[pl.ds(b * LANES, LANES)], sems.at[b - start])
            )
            copies[-1].start()
            b += 1
    for copy in copies:
        copy.wait()


def run_update(layer, start, buffer, angulars, bonds, gates, weight):
    per, slots, channels, _ = bonds.shape
    parts = len(angulars)
    return pl.pallas_call(
        functools.partial(update_kernel, layer, start, slots, channels, parts),
        out_shape=jax.ShapeDtypeStruct((per * LANES, slots * channels), BF),
        in_specs=[VMEM] * (parts + 3) + [ANY],
        out_specs=ANY,
        input_output_aliases={} if buffer is None else {parts + 3: 0},
        scratch_shapes=[
            pltpu.VMEM((channels, channels), BF),
            pltpu.VMEM((per, LANES, slots * channels), BF),
            pltpu.SemaphoreType.DMA((per,)),
        ],
        compiler_params=PARAMS,
        cost_estimate=pl.CostEstimate(flops=2**30, bytes_accessed=2**23, transcendentals=0),
    )(*angulars, bonds, gates, weight, weight if buffer is None else buffer)


def passed_along(value, steps):
    count = lax.axis_size(AXES)
    return lax.ppermute(value, AXES, [(source, (source + steps) % count) for source in range(count)])


def edge_kernel(domain_ref, payload_ref):
    rim = payload_ref.shape[1]
    start = jnp.where(lax.axis_index("rep") < 2, domain_ref.shape[1] - rim, 0)
    payload_ref[...] = domain_ref[:, pl.ds(pl.multiple_of(start, LANES), rim)].astype(BF)


def far_side(domain, quarter):
    rim = 2 * quarter
    rep = lax.axis_size("rep")
    total = lax.axis_size(AXES)
    payload = pl.pallas_call(
        edge_kernel,
        out_shape=jax.ShapeDtypeStruct((domain.shape[0], rim), BF),
        in_specs=[VMEM],
        out_specs=VMEM,
        compiler_params=PARAMS,
        cost_estimate=pl.CostEstimate(flops=10 * 2**30, bytes_accessed=2**23, transcendentals=2**22),
    )(domain)
    pairs = []
    for start in range(0, total, rep):
        for d in range(rep):
            pairs.append(((start + d + (-rep if d < 2 else rep)) % total, start + d))
    return lax.ppermute(payload, AXES, pairs)


def sum_stages():
    def exchange(axis, step):
        size = lax.axis_size(axis)
        return lambda value: value + lax.ppermute(value, axis, [(i, i ^ step) for i in range(size)])

    return [
        exchange(axis, 1 << bit)
        for axis in ("space", "rep")
        for bit in reversed(range(lax.axis_size(axis).bit_length() - 1))
    ]


def per_device(
    atom_features,
    bond_features,
    offsets,
    counts,
    cosines,
    weight_core,
    weight_atom,
    weight_pair,
    weight_cosine,
    weight_bond,
    weight_energy,
):
    quarter = offsets.shape[0]
    per = quarter // LANES
    domain = atom_features.T
    offs = offsets.T
    cnts = counts[None, :]
    into_atoms = (weight_core, weight_atom)
    into_angles = (weight_pair, weight_cosine)
    shape = (per, offsets.shape[1], domain.shape[0], LANES)
    far = far_side(domain, quarter)
    angular, bonds, tiles, later_p, later_q = run_angle(0, True, 0, EARLY, bond_features, cnts, cosines, into_angles, shape)
    state, gates, table, late = run_gather(
        0, [domain, far], None, bonds, offs, cnts, into_atoms, [weight_cosine, tiles, later_p, later_q]
    )
    pieces = [table if s == 0 else passed_along(table, s) for s in (2, 1, 0, -1, -2)]
    bonds = run_inner_update(0, [angular, late], bonds, gates, weight_bond)
    angulars = [run_angle(1, False, b, 1, bonds, cnts, tiles, into_angles, shape)[0] for b in range(HIDING)]
    state, gates, energy = run_gather(
        1, pieces, state, bonds, offs, cnts, into_atoms, [weight_energy[None, :], angulars[-1]]
    )
    stages = sum_stages()
    for part in range(HIDING, per):
        if stages:
            energy = stages.pop(0)(energy)
        angulars += run_angle(1, False, part, 1, bonds, cnts, tiles, into_angles, shape)
    out = None
    half = per // 2
    for part in range(2):
        if stages:
            energy = stages.pop(0)(energy)
        mine = angulars[part * half : (part + 1) * half]
        out = run_update(1, part * half, out, mine, bonds, gates, weight_bond)
    for stage in stages:
        energy = stage(energy)
    scale = math.sqrt(lax.axis_size("space") * domain.shape[1])
    return (state.T, out, jnp.sum(energy) / scale)


def solution(mesh):
    return jax.shard_map(
        per_device,
        mesh=mesh,
        in_specs=(
            P("space", None),
            P(("space", "rep"), None),
            P(("space", "rep"), None),
            P(("space", "rep")),
            P(("space", "rep"), None),
            P(),
            P(),
            P(),
            P(),
            P(),
            P(),
        ),
        out_specs=(P(("space", "rep"), None), P(("space", "rep"), None), P()),
        check_vma=False,
    )
```
